32 devices in a mesh: sta: 32 (over z, y, x, core).
Axes of the slice: x: 2, y: 2, z: 4, core: 2. Of those that a mesh axis runs over, the one named last changes fastest.
Arguments:
- records: bfloat16 [2560, 2048], P('sta'), may hold values from -6 to 6
- green: bfloat16 [2560, 2048], P('sta'), may hold values from -4 to 4
- pair_mask: int32 [2560, 720], P('sta'), may hold values 0 or 1
- tile_lists: int32 [2560, 16], P('sta'), may hold values from 0 to 127
- tile_weights: float32 [2560, 16], P('sta'), may hold values from -0.3125 to 0.3125
- tile_green: bfloat16 [65536, 1024], P('sta'), may hold values from -0.125 to 0.125
Outputs:
- adjoint: bfloat16 [2560, 2048], P('sta')
- kernel: float32 [128, 1024], P('sta')
The draws below stay inside these ranges and needn't reach their ends.
All inputs are finite; a program needn't handle non-finite values. No bound on the sum of `pair_mask` on one device may be relied on, other than what follows from the above.
Results may differ from the reference program's by a relative error of at most 0.0034.
Values may be sent and summed in bfloat16 or wider, within the bound.
A program may use at most 64 MiB of HBM per device.

```python
import jax
import jax.numpy as jnp
from jax import lax

C = 80
F = 1024
CT = 1024
TT = 4
L = 16
HALF = 4
WIN = 9
CHANNELS = 2560
TILES = 128
N_STA = 32


def place_ends(values, stream_key, smallest, top_value):
    extent = values.shape
    spot = [jax.random.randint(jax.random.fold_in(stream_key, axis), (), 0, extent[axis]) for axis in range(len(extent))]
    values = values.at[tuple(spot)].set(smallest)
    longest = extent.index(max(extent))
    spot[longest] = (spot[longest] + 1) % extent[longest]
    return values.at[tuple(spot)].set(top_value)


def block_scale(own_key, extent, shards, least, high):
    def one(position, blocks):
        steps = jax.random.uniform(jax.random.fold_in(jax.random.fold_in(own_key, 6), position), (blocks,), jnp.float32, least / len(shards), high / len(shards))
        return jnp.repeat(jnp.exp(steps), extent[position] // blocks).reshape((-1,) + (1,) * (len(extent) - position - 1))

    gain = one(*shards[0])
    for cut in shards[1:]:
        gain = gain * one(*cut)
    return gain


def bell_draw(key, extent, width, limit, shards=(), kind=jnp.bfloat16):
    result = jax.random.normal(key, extent, jnp.float32) * width
    if len(shards) > 0:
        result = block_scale(key, extent, shards, -0.22, 0.18) * result
    return jnp.clip(result, min=-limit, max=limit).astype(kind)


def setup_inputs(seed: int = 0) -> dict:
    key_list = jax.random.split(jax.random.key(seed), 7)
    records = bell_draw(key_list[0], (CHANNELS, 2 * F), 1.0, 6.0, ((0, 32),))
    green = bell_draw(key_list[1], (CHANNELS, 2 * F), 0.6, 4.0, ((0, 32),))
    pair_mask = place_ends((jax.random.randint(key_list[2], (CHANNELS, WIN * C), 0, 2) < 1).astype(jnp.int32), jax.random.fold_in(key_list[2], 1), 0, 1)
    tile_lists = place_ends(jax.random.randint(key_list[3], (CHANNELS, L), 0, TILES), jax.random.fold_in(key_list[3], 1), 0, TILES - 1).astype(jnp.int32)
    tile_weights = bell_draw(key_list[4], (CHANNELS, L), (C * L // TT) ** -0.5, 0.3125, ((0, 32),), jnp.float32)
    tile_green = bell_draw(key_list[5], (2 * F * N_STA, CT), (2 * F) ** -0.5, 0.125, ((0, 32),))
    return {"records": records, "green": green, "pair_mask": pair_mask, "tile_lists": tile_lists, "tile_weights": tile_weights, "tile_green": tile_green}


def reference(records, green, pair_mask, tile_lists, tile_weights, tile_green):
    blocks = N_STA
    rec = records.astype(jnp.float32)
    grn = green.astype(jnp.float32)
    rec_real, rec_imag = (rec[:, :F], rec[:, F:])
    green_real, green_imag = (grn[:, :F], grn[:, F:])
    cross = jnp.concatenate([rec_real * green_real + rec_imag * green_imag, rec_real * green_imag - rec_imag * green_real], axis=1).astype(jnp.bfloat16)
    power = (green_real * green_real + green_imag * green_imag).astype(jnp.bfloat16)
    cross_blocks = cross.astype(jnp.float32).reshape(blocks, C, 2 * F)
    power_blocks = power.astype(jnp.float32).reshape(blocks, C, F)
    mask_blocks = pair_mask.astype(jnp.float32).reshape(blocks, C, WIN, C)
    qsum = jnp.zeros((blocks, C, 2 * F), jnp.float32)
    psum = jnp.zeros((blocks, C, F), jnp.float32)
    for offset in range(WIN):
        rolled_cross = jnp.roll(cross_blocks, HALF - offset, axis=0)
        rolled_power = jnp.roll(power_blocks, HALF - offset, axis=0)
        qsum = qsum + jnp.einsum('bic,bcf->bif', mask_blocks[:, :, offset, :], rolled_cross, precision=lax.Precision.HIGHEST)
        psum = psum + jnp.einsum('bic,bcf->bif', mask_blocks[:, :, offset, :], rolled_power, precision=lax.Precision.HIGHEST)
    factor = 1.0 / jnp.sqrt(jnp.float32(WIN * C))
    qsum = (qsum * factor).reshape(blocks * C, 2 * F)
    psum = (psum * factor).reshape(blocks * C, F)
    q_real, q_imag = (qsum[:, :F], qsum[:, F:])
    adj_real = rec_real * q_real - rec_imag * q_imag - green_real * psum
    adj_imag = rec_real * q_imag + rec_imag * q_real - green_imag * psum
    adjoint = jnp.concatenate([adj_real, adj_imag], axis=1).astype(jnp.bfloat16)
    tiles_total = TT * blocks
    tile_ids = jnp.arange(tiles_total, dtype=jnp.int32)

    def one_block(total, inputs):
        adj_rows, lists_rows, weight_rows, green_rows = inputs
        onehot = (lists_rows[None, :, :] == tile_ids[:, None, None]).astype(jnp.float32)
        tile_map = lax.optimization_barrier(jnp.sum(onehot * weight_rows[None, :, :], axis=2))
        spread = jnp.dot(tile_map, adj_rows.astype(jnp.float32), precision=lax.Precision.HIGHEST)
        return (total + jnp.dot(spread, green_rows.astype(jnp.float32), precision=lax.Precision.HIGHEST), None)
    inputs = (adjoint.reshape(blocks, C, 2 * F), tile_lists.reshape(blocks, C, L), tile_weights.reshape(blocks, C, L), tile_green.reshape(blocks, 2 * F, CT))
    kernel, unused = lax.scan(one_block, jnp.zeros((tiles_total, CT), jnp.float32), inputs)
    return (adjoint, kernel)
```

```python
import functools

import jax
import jax.numpy as jnp
from jax import lax
from jax.experimental import pallas as pl
from jax.experimental.pallas import tpu as pltpu
from jax.sharding import PartitionSpec as P

C = 80
F = 1024
TT = 4
WIN = 9
CT = 1024
Q = 4
FC = F // Q
MB = 4
MESH = pl.DeviceIdType.MESH

X, Y, Z, V, T, PEER = 0, 1, 2, 3, 4, 5
KINDS = 9
TRANSIT = WIN


def body(
    n, rec, grn, mask, lists, weights, tg_hbm, adj_out, ker_out,
    buf, mask_bf, tg, w_acc, terms, halves, wide, packed, landed,
    send_sem, recv_sem, tg_sem, half_sem, sum_sem,
):
    chips = n // 2
    planes = n // 8
    half = TT * chips
    me = lax.axis_index("sta")
    core = lax.rem(me, 2)
    chip = me // 2
    j = lax.rem(chip, 4)
    plane = me // 8
    odd = lax.rem(j, 2)
    upper = j // 2
    inner = lax.rem((j + 1) // 2, 2)
    peer = me + 1 - 2 * core
    x_dev = me + 2 - 4 * odd
    y_dev = me + 4 - 8 * upper
    z_dev = lax.rem(plane + 1 - 2 * upper + planes, planes) * 8 + lax.rem(me, 8)
    slot_x = 6 - 4 * odd
    slot_v = 2 + 4 * odd
    slot_y = 8 - 8 * upper
    slot_z = 8 * upper
    is0 = core == 0
    is1 = core == 1

    barrier = pltpu.get_barrier_semaphore()
    pl.semaphore_signal(barrier, inc=1, device_id=(peer,), device_id_type=MESH)

    @pl.loop(1, chips)
    def _(o):
        other = lax.rem(chip + o, chips) * 2 + core
        pl.semaphore_signal(barrier, inc=1, device_id=(other,), device_id_type=MESH)

    tg_copy = pltpu.make_async_copy(tg_hbm, tg, tg_sem)
    tg_copy.start()

    def part(ref, q, imag):
        return ref[:, imag * F + q * FC : imag * F + (q + 1) * FC].astype(jnp.float32)

    def fill(q):
        dr, di = part(rec, q, 0), part(rec, q, 1)
        gr, gi = part(grn, q, 0), part(grn, q, 1)
        buf[q, 4, :, 0:FC] = (dr * gr + di * gi).astype(jnp.bfloat16)
        buf[q, 4, :, FC : 2 * FC] = (dr * gi - di * gr).astype(jnp.bfloat16)
        buf[q, 4, :, 2 * FC : 3 * FC] = (gr * gr + gi * gi).astype(jnp.bfloat16)

    def move(q, src, dst, sender, kind, device):
        return pltpu.make_async_remote_copy(
            src_ref=buf.at[q, src], dst_ref=buf.at[q, dst],
            send_sem=send_sem.at[q, sender], recv_sem=recv_sem.at[q, kind],
            device_id=(device,), device_id_type=MESH,
        )

    def relay(q, src, which):
        return move(q, src, src + 2 * core - 1, PEER + which, PEER + which, peer)

    def arrived(q, slot, kind):
        move(q, slot, slot, kind, kind, peer).wait_recv()

    def sent(q, kind):
        move(q, 4, 4, kind, kind, peer).wait_send()

    def send_own(q):
        move(q, 4, slot_z, Y, Y, y_dev).start()
        move(q, 4, slot_v, X, X, x_dev).start()
        relay(q, 4, 0).start()

    def stage1(q):
        arrived(q, slot_y, Y)
        move(q, slot_y, slot_z, Z, Z, z_dev).start()

        @pl.when(core == upper)
        def _():
            relay(q, slot_y, 3).start()

        @pl.when(is0 & (inner == 0))
        def _():
            move(q, slot_y, slot_x, V, V, x_dev).start()

        arrived(q, slot_x, X)

        @pl.when(is1 & (inner == 0))
        def _():
            move(q, slot_x, slot_v, V, V, y_dev).start()

        @pl.when(is1 & (inner == 1))
        def _():
            move(q, slot_x, TRANSIT, V, T, y_dev).start()

        relay(q, slot_x, 1).start()

    def stage2(q):
        @pl.when(is1 & (inner == 0))
        def _():
            arrived(q, TRANSIT, T)
            move(q, TRANSIT, slot_v, T, V, z_dev).start()

        arrived(q, slot_z, Z)

        @pl.when(is0 & (inner == 1))
        def _():
            move(q, slot_z, slot_x, V, V, x_dev).start()

        @pl.when(core != upper)
        def _():
            relay(q, slot_z, 3).start()

    def stage3(q):
        arrived(q, slot_v, V)
        relay(q, slot_v, 2).start()

    def peer_slot(slot):
        return slot + 1 - 2 * core

    def stage4(q):
        arrived(q, peer_slot(4), PEER)
        arrived(q, peer_slot(slot_x), PEER + 1)
        arrived(q, peer_slot(slot_v), PEER + 2)
        theirs = 8 * core
        arrived(q, peer_slot(theirs), PEER + 3)
        window = buf[q, 0:WIN].reshape(WIN * C, 3 * FC)
        sums = jnp.dot(mask_bf[...], window, preferred_element_type=jnp.float32)
        sums = sums * (1.0 / jnp.sqrt(jnp.float32(WIN * C)))
        q_real, q_imag, p = sums[:, :FC], sums[:, FC : 2 * FC], sums[:, 2 * FC :]
        dr, di = part(rec, q, 0), part(rec, q, 1)
        gr, gi = part(grn, q, 0), part(grn, q, 1)
        real = (dr * q_real - di * q_imag - gr * p).astype(jnp.bfloat16)
        imag = (dr * q_imag + di * q_real - gi * p).astype(jnp.bfloat16)
        adj_out[:, q * FC : (q + 1) * FC] = real
        adj_out[:, F + q * FC : F + (q + 1) * FC] = imag
        if q == 0:
            tg_copy.wait()
        more = jnp.dot(
            real, tg[q * FC : (q + 1) * FC, :], preferred_element_type=jnp.float32
        ) + jnp.dot(
            imag, tg[F + q * FC : F + (q + 1) * FC, :], preferred_element_type=jnp.float32
        )
        w_acc[...] = more if q == 0 else w_acc[...] + more

    fill(0)
    pl.semaphore_wait(barrier, chips)
    send_own(0)
    for q in range(1, Q):
        fill(q)
        send_own(q)

    mask_bf[...] = mask[...].astype(jnp.float32).astype(jnp.bfloat16)
    row = lax.broadcasted_iota(jnp.int32, (2 * half, C), 0)
    late = jnp.where(row >= half, 1, 0)
    rest = row - half * late
    tile = (rest >> 2) * (2 * TT) + late * TT + (rest & 3)
    tile_map = jnp.zeros((2 * half, C), jnp.float32)
    for l in range(lists.shape[0]):
        tile_map = tile_map + jnp.where(lists[l : l + 1, :] == tile, weights[l : l + 1, :], 0.0)
    map_high = tile_map.astype(jnp.bfloat16)
    map_low = (tile_map - map_high.astype(jnp.float32)).astype(jnp.bfloat16)

    for step in range(Q + 3):
        if step < Q:
            stage1(step)
        if 0 <= step - 1 < Q:
            stage2(step - 1)
        if 0 <= step - 2 < Q:
            stage3(step - 2)
        if 0 <= step - 3 < Q:
            stage4(step - 3)

    w = w_acc[...]
    w_high = w.astype(jnp.bfloat16)
    w_low = (w - w_high.astype(jnp.float32)).astype(jnp.bfloat16)
    terms[...] = (
        jnp.dot(map_high, w_high, preferred_element_type=jnp.float32)
        + jnp.dot(map_high, w_low, preferred_element_type=jnp.float32)
        + jnp.dot(map_low, w_high, preferred_element_type=jnp.float32)
    )
    to_peer = pltpu.make_async_remote_copy(
        src_ref=terms.at[pl.ds(pl.multiple_of((1 - core) * half, half), half)], dst_ref=halves,
        send_sem=half_sem.at[0], recv_sem=half_sem.at[1],
        device_id=(peer,), device_id_type=MESH,
    )
    to_peer.start()
    to_peer.wait_recv()
    width = CT // MB

    @pl.loop(0, chips // 2)
    def _(i):
        start = pl.multiple_of(8 * i, 8)
        both = terms[pl.ds(pl.multiple_of(core * half + start, 8), 8), :] + halves[pl.ds(start, 8), :]
        for m in range(MB):
            cols = both[:, m * width : (m + 1) * width]
            wide[2 * i, m * TT : (m + 1) * TT, :] = cols[0:TT]
            wide[2 * i + 1, m * TT : (m + 1) * TT, :] = cols[TT : 2 * TT]
        packed[2 * i] = wide[2 * i].astype(jnp.bfloat16)
        packed[2 * i + 1] = wide[2 * i + 1].astype(jnp.bfloat16)

    def piece(o):
        other = lax.rem(chip + o, chips)
        return pltpu.make_async_remote_copy(
            src_ref=packed.at[other], dst_ref=landed.at[o - 1],
            send_sem=sum_sem.at[0], recv_sem=sum_sem.at[1],
            device_id=(other * 2 + core,), device_id_type=MESH,
        )

    @pl.loop(1, chips)
    def _(o):
        piece(o).start()

    for q in range(Q):
        sent(q, X)
        sent(q, Y)
        sent(q, Z)
        for which in range(4):
            sent(q, PEER + which)

        sent(q, V)

        @pl.when(is1 & (inner == 0))
        def _():
            sent(q, T)

    to_peer.wait_send()
    everything = pltpu.make_async_remote_copy(
        src_ref=packed.at[0 : chips - 1], dst_ref=landed,
        send_sem=sum_sem.at[0], recv_sem=sum_sem.at[1],
        device_id=(peer,), device_id_type=MESH,
    )
    everything.wait_recv()
    total = lax.fori_loop(
        0, chips - 1, lambda o, t: t + landed[o].astype(jnp.float32), wide[chip]
    )
    for m in range(MB):
        ker_out[:, m * width : (m + 1) * width] = total[m * TT : (m + 1) * TT]
    everything.wait_send()


def local(n, records, green, pair_mask, tile_lists, tile_weights, tile_green):
    chips = n // 2
    half = TT * chips
    vmem = pl.BlockSpec(memory_space=pltpu.VMEM)
    return pl.pallas_call(
        functools.partial(body, n),
        out_shape=(
            jax.ShapeDtypeStruct((C, 2 * F), jnp.bfloat16),
            jax.ShapeDtypeStruct((TT, CT), jnp.float32),
        ),
        in_specs=[vmem] * 5 + [pl.BlockSpec(memory_space=pl.ANY)],
        out_specs=(vmem, vmem),
        scratch_shapes=[
            pltpu.VMEM((Q, WIN + 1, C, 3 * FC), jnp.bfloat16),
            pltpu.VMEM((C, WIN * C), jnp.bfloat16),
            pltpu.VMEM((2 * F, CT), jnp.bfloat16),
            pltpu.VMEM((C, CT), jnp.float32),
            pltpu.VMEM((2 * half, CT), jnp.float32),
            pltpu.VMEM((half, CT), jnp.float32),
            pltpu.VMEM((chips, MB * TT, CT // MB), jnp.float32),
            pltpu.VMEM((chips, MB * TT, CT // MB), jnp.bfloat16),
            pltpu.VMEM((chips - 1, MB * TT, CT // MB), jnp.bfloat16),
            pltpu.SemaphoreType.DMA((Q, KINDS)),
            pltpu.SemaphoreType.DMA((Q, KINDS)),
            pltpu.SemaphoreType.DMA,
            pltpu.SemaphoreType.DMA((2,)),
            pltpu.SemaphoreType.DMA((2,)),
        ],
        compiler_params=pltpu.CompilerParams(
            collective_id=0, has_side_effects=True, vmem_limit_bytes=44 * 2**20
        ),
        cost_estimate=pl.CostEstimate(flops=10**9, bytes_accessed=6 * 10**6, transcendentals=0),
    )(records, green, pair_mask, tile_lists.T, tile_weights.T, tile_green)


def solution(mesh):
    n = mesh.shape["sta"]
    return jax.shard_map(
        functools.partial(local, n),
        mesh=mesh,
        in_specs=(P("sta", None),) * 6,
        out_specs=(P("sta", None), P("sta", None)),
        check_vma=False,
    )
```

```python
import functools

import jax
import jax.numpy as jnp
from jax import lax
from jax.experimental import pallas as pl
from jax.experimental.pallas import tpu as pltpu
from jax.sharding import PartitionSpec as P

C = 80
F = 1024
TT = 4
WIN = 9
CT = 1024
Q = 8
FC = F // Q
AHEAD = 2
MB = 4
MESH = pl.DeviceIdType.MESH

X, Y, Z, V, T, PEER = 0, 1, 2, 3, 4, 5
KINDS = 9
TRANSIT = WIN


def body(
    n, rec_hbm, grn_hbm, mask_hbm, lists_hbm, weights_hbm, tg_hbm, adj_hbm, ker_out,
    adj_out, rec, grn, mask, lists, weights, buf, mask_bf, map_all, tg, w_acc, terms, halves, wide, packed, landed,
    send_sem, recv_sem, in_sem, half_sem, sum_sem,
):
    chips = n // 2
    planes = n // 8
    half = TT * chips
    me = lax.axis_index("sta")
    core = lax.rem(me, 2)
    chip = me // 2
    j = lax.rem(chip, 4)
    plane = me // 8
    odd = lax.rem(j, 2)
    upper = j // 2
    inner = lax.rem((j + 1) // 2, 2)
    peer = me + 1 - 2 * core
    x_dev = me + 2 - 4 * odd
    y_dev = me + 4 - 8 * upper
    z_dev = lax.rem(plane + 1 - 2 * upper + planes, planes) * 8 + lax.rem(me, 8)
    slot_x = 6 - 4 * odd
    slot_v = 2 + 4 * odd
    slot_y = 8 - 8 * upper
    slot_z = 8 * upper
    is0 = core == 0
    is1 = core == 1

    fetches = [
        pltpu.make_async_copy(src, dst, in_sem.at[i])
        for i, (src, dst) in enumerate(
            (
                (rec_hbm, rec), (grn_hbm, grn), (mask_hbm, mask),
                (lists_hbm, lists), (weights_hbm, weights), (tg_hbm, tg),
            )
        )
    ]
    fetches[0].start()
    fetches[1].start()
    barrier = pltpu.get_barrier_semaphore()
    pl.semaphore_signal(barrier, inc=1, device_id=(peer,), device_id_type=MESH)

    @pl.loop(1, chips)
    def _(o):
        other = lax.rem(chip + o, chips) * 2 + core
        pl.semaphore_signal(barrier, inc=1, device_id=(other,), device_id_type=MESH)

    for fetch in fetches[2:]:
        fetch.start()

    def part(ref, q, imag):
        return ref[:, imag * F + q * FC : imag * F + (q + 1) * FC].astype(jnp.float32)

    def fill(q):
        dr, di = part(rec, q, 0), part(rec, q, 1)
        gr, gi = part(grn, q, 0), part(grn, q, 1)
        buf[q, 4, :, 0:FC] = (dr * gr + di * gi).astype(jnp.bfloat16)
        buf[q, 4, :, FC : 2 * FC] = (dr * gi - di * gr).astype(jnp.bfloat16)
        buf[q, 4, :, 2 * FC : 3 * FC] = (gr * gr + gi * gi).astype(jnp.bfloat16)

    def move(q, src, dst, sender, kind, device):
        return pltpu.make_async_remote_copy(
            src_ref=buf.at[q, src], dst_ref=buf.at[q, dst],
            send_sem=send_sem.at[q, sender], recv_sem=recv_sem.at[q, kind],
            device_id=(device,), device_id_type=MESH,
        )

    def relay(q, src, which):
        return move(q, src, src + 2 * core - 1, PEER + which, PEER + which, peer)

    def arrived(q, slot, kind):
        move(q, slot, slot, kind, kind, peer).wait_recv()

    def sent(q, kind):
        move(q, 4, 4, kind, kind, peer).wait_send()

    def send_own(q):
        move(q, 4, slot_z, Y, Y, y_dev).start()
        move(q, 4, slot_v, X, X, x_dev).start()
        relay(q, 4, 0).start()

    def stage1(q):
        arrived(q, slot_y, Y)
        move(q, slot_y, slot_z, Z, Z, z_dev).start()

        @pl.when(core == upper)
        def _():
            relay(q, slot_y, 3).start()

        @pl.when(is0 & (inner == 0))
        def _():
            move(q, slot_y, slot_x, V, V, x_dev).start()

        arrived(q, slot_x, X)

        @pl.when(is1 & (inner == 0))
        def _():
            move(q, slot_x, slot_v, V, V, y_dev).start()

        @pl.when(is1 & (inner == 1))
        def _():
            move(q, slot_x, TRANSIT, V, T, y_dev).start()

        relay(q, slot_x, 1).start()

    def stage2(q):
        @pl.when(is1 & (inner == 0))
        def _():
            arrived(q, TRANSIT, T)
            move(q, TRANSIT, slot_v, T, V, z_dev).start()

        arrived(q, slot_z, Z)

        @pl.when(is0 & (inner == 1))
        def _():
            move(q, slot_z, slot_x, V, V, x_dev).start()

        @pl.when(core != upper)
        def _():
            relay(q, slot_z, 3).start()

    def stage3(q):
        arrived(q, slot_v, V)
        relay(q, slot_v, 2).start()

    def peer_slot(slot):
        return slot + 1 - 2 * core

    def stage4(q):
        arrived(q, peer_slot(4), PEER)
        arrived(q, peer_slot(slot_x), PEER + 1)
        arrived(q, peer_slot(slot_v), PEER + 2)
        theirs = 8 * core
        arrived(q, peer_slot(theirs), PEER + 3)
        window = buf[q, 0:WIN].reshape(WIN * C, 3 * FC)
        sums = jnp.dot(mask_bf[...], window, preferred_element_type=jnp.float32)
        sums = sums * (1.0 / jnp.sqrt(jnp.float32(WIN * C)))
        q_real, q_imag, p = sums[:, :FC], sums[:, FC : 2 * FC], sums[:, 2 * FC :]
        dr, di = part(rec, q, 0), part(rec, q, 1)
        gr, gi = part(grn, q, 0), part(grn, q, 1)
        real = (dr * q_real - di * q_imag - gr * p).astype(jnp.bfloat16)
        imag = (dr * q_imag + di * q_real - gi * p).astype(jnp.bfloat16)
        adj_out[:, q * FC : (q + 1) * FC] = real
        adj_out[:, F + q * FC : F + (q + 1) * FC] = imag
        if q == 0:
            fetches[5].wait()
        more = jnp.dot(
            real, tg[q * FC : (q + 1) * FC, :], preferred_element_type=jnp.float32
        ) + jnp.dot(
            imag, tg[F + q * FC : F + (q + 1) * FC, :], preferred_element_type=jnp.float32
        )
        w_acc[...] = more if q == 0 else w_acc[...] + more

    fetches[0].wait()
    fetches[1].wait()
    fill(0)
    pl.semaphore_wait(barrier, chips)
    send_own(0)
    for q in range(1, Q):
        fill(q)
        if q < AHEAD:
            send_own(q)

    for fetch in fetches[2:5]:
        fetch.wait()
    mask_bf[...] = mask[...].astype(jnp.float32).astype(jnp.bfloat16)
    row = lax.broadcasted_iota(jnp.int32, (2 * half, C), 0)
    late = jnp.where(row >= half, 1, 0)
    rest = row - half * late
    tile = (rest >> 2) * (2 * TT) + late * TT + (rest & 3)
    tile_map = jnp.zeros((2 * half, C), jnp.float32)
    for l in range(lists.shape[0]):
        tile_map = tile_map + jnp.where(lists[l : l + 1, :] == tile, weights[l : l + 1, :], 0.0)
    map_high = tile_map.astype(jnp.bfloat16)
    map_low = (tile_map - map_high.astype(jnp.float32)).astype(jnp.bfloat16)
    map_all[...] = jnp.concatenate([map_high, map_high, map_low], axis=1)

    for step in range(Q + 3):
        if step < Q:
            stage1(step)
        if step + AHEAD < Q:
            send_own(step + AHEAD)
        if 0 <= step - 1 < Q:
            stage2(step - 1)
        if 0 <= step - 2 < Q:
            stage3(step - 2)
        if 0 <= step - 3 < Q:
            stage4(step - 3)

    adj_copy = pltpu.make_async_copy(adj_out, adj_hbm, in_sem.at[6])
    adj_copy.start()

    w = w_acc[...]
    w_high = w.astype(jnp.bfloat16)
    w_low = (w - w_high.astype(jnp.float32)).astype(jnp.bfloat16)
    w_all = jnp.concatenate([w_high, w_low, w_high], axis=0)
    terms[...] = jnp.dot(map_all[...], w_all, preferred_element_type=jnp.float32)
    to_peer = pltpu.make_async_remote_copy(
        src_ref=terms.at[pl.ds(pl.multiple_of((1 - core) * half, half), half)], dst_ref=halves,
        send_sem=half_sem.at[0], recv_sem=half_sem.at[1],
        device_id=(peer,), device_id_type=MESH,
    )
    to_peer.start()
    to_peer.wait_recv()
    width = CT // MB

    @pl.loop(0, chips // 2)
    def _(i):
        start = pl.multiple_of(8 * i, 8)
        both = terms[pl.ds(pl.multiple_of(core * half + start, 8), 8), :] + halves[pl.ds(start, 8), :]
        for m in range(MB):
            cols = both[:, m * width : (m + 1) * width]
            wide[2 * i, m * TT : (m + 1) * TT, :] = cols[0:TT]
            wide[2 * i + 1, m * TT : (m + 1) * TT, :] = cols[TT : 2 * TT]
        packed[2 * i] = wide[2 * i].astype(jnp.bfloat16)
        packed[2 * i + 1] = wide[2 * i + 1].astype(jnp.bfloat16)

    def piece(o):
        other = lax.rem(chip + o, chips)
        return pltpu.make_async_remote_copy(
            src_ref=packed.at[other], dst_ref=landed.at[o - 1],
            send_sem=sum_sem.at[0], recv_sem=sum_sem.at[1],
            device_id=(other * 2 + core,), device_id_type=MESH,
        )

    @pl.loop(1, chips)
    def _(o):
        piece(o).start()

    for q in range(Q):
        sent(q, X)
        sent(q, Y)
        sent(q, Z)
        for which in range(4):
            sent(q, PEER + which)

        sent(q, V)

        @pl.when(is1 & (inner == 0))
        def _():
            sent(q, T)

    to_peer.wait_send()
    everything = pltpu.make_async_remote_copy(
        src_ref=packed.at[0 : chips - 1], dst_ref=landed,
        send_sem=sum_sem.at[0], recv_sem=sum_sem.at[1],
        device_id=(peer,), device_id_type=MESH,
    )
    everything.wait_recv()
    total = lax.fori_loop(
        0, chips - 1, lambda o, t: t + landed[o].astype(jnp.float32), wide[chip]
    )
    for m in range(MB):
        ker_out[:, m * width : (m + 1) * width] = total[m * TT : (m + 1) * TT]
    everything.wait_send()
    adj_copy.wait()


def hand_over(adj, ker, adj_out, ker_out, sem):
    first = pltpu.make_async_copy(adj, adj_out, sem.at[0])
    second = pltpu.make_async_copy(ker, ker_out, sem.at[1])
    first.start()
    second.start()
    first.wait()
    second.wait()


def local(n, records, green, pair_mask, tile_lists, tile_weights, tile_green):
    chips = n // 2
    half = TT * chips
    vmem = pl.BlockSpec(memory_space=pltpu.VMEM)
    hbm = pl.BlockSpec(memory_space=pltpu.HBM)
    adjoint, kernel = pl.pallas_call(
        functools.partial(body, n),
        out_shape=(
            jax.ShapeDtypeStruct((C, 2 * F), jnp.bfloat16),
            jax.ShapeDtypeStruct((TT, CT), jnp.float32),
        ),
        in_specs=[hbm] * 6,
        out_specs=(hbm, vmem),
        scratch_shapes=[
            pltpu.VMEM((C, 2 * F), jnp.bfloat16),
            pltpu.VMEM(records.shape, records.dtype),
            pltpu.VMEM(green.shape, green.dtype),
            pltpu.VMEM(pair_mask.shape, pair_mask.dtype),
            pltpu.VMEM(tile_lists.shape[::-1], tile_lists.dtype),
            pltpu.VMEM(tile_weights.shape[::-1], tile_weights.dtype),
            pltpu.VMEM((Q, WIN + 1, C, 3 * FC), jnp.bfloat16),
            pltpu.VMEM((C, WIN * C), jnp.bfloat16),
            pltpu.VMEM((2 * half, 3 * C), jnp.bfloat16),
            pltpu.VMEM((2 * F, CT), jnp.bfloat16),
            pltpu.VMEM((C, CT), jnp.float32),
            pltpu.VMEM((2 * half, CT), jnp.float32),
            pltpu.VMEM((half, CT), jnp.float32),
            pltpu.VMEM((chips, MB * TT, CT // MB), jnp.float32),
            pltpu.VMEM((chips, MB * TT, CT // MB), jnp.bfloat16),
            pltpu.VMEM((chips - 1, MB * TT, CT // MB), jnp.bfloat16),
            pltpu.SemaphoreType.DMA((Q, KINDS)),
            pltpu.SemaphoreType.DMA((Q, KINDS)),
            pltpu.SemaphoreType.DMA((7,)),
            pltpu.SemaphoreType.DMA((2,)),
            pltpu.SemaphoreType.DMA((2,)),
        ],
        compiler_params=pltpu.CompilerParams(
            collective_id=0, has_side_effects=True, vmem_limit_bytes=56 * 2**20
        ),
        cost_estimate=pl.CostEstimate(flops=10**9, bytes_accessed=6 * 10**6, transcendentals=0),
    )(records, green, pair_mask, tile_lists.T, tile_weights.T, tile_green)
    return pl.pallas_call(
        hand_over,
        out_shape=(
            jax.ShapeDtypeStruct(adjoint.shape, adjoint.dtype),
            jax.ShapeDtypeStruct(kernel.shape, kernel.dtype),
        ),
        in_specs=[hbm] * 2,
        out_specs=(hbm, hbm),
        scratch_shapes=[pltpu.SemaphoreType.DMA((2,))],
    )(adjoint, kernel)


def solution(mesh):
    n = mesh.shape["sta"]
    return jax.shard_map(
        functools.partial(local, n),
        mesh=mesh,
        in_specs=(P("sta", None),) * 6,
        out_specs=(P("sta", None), P("sta", None)),
        check_vma=False,
    )
```

```python
import functools

import jax
import jax.numpy as jnp
from jax import lax
from jax.experimental import pallas as pl
from jax.experimental.pallas import tpu as pltpu
from jax.sharding import PartitionSpec as P

C = 80
F = 1024
TT = 4
WIN = 9
CT = 1024
Q = 8
FC = F // Q
AHEAD = 3
LAGS = 2, 4, 6
MB = 4
MESH = pl.DeviceIdType.MESH

X, Y, Z, V, T, PEER = 0, 1, 2, 3, 4, 5
KINDS = 9
TRANSIT = WIN


def body(
    n, rec_hbm, grn_hbm, mask_hbm, lists_hbm, weights_hbm, tg_hbm, adj_hbm, ker_out,
    adj_out, rec, grn, mask, lists, weights, buf, mask_bf, map_all, tg, w_acc, terms, halves, wide, packed, landed,
    send_sem, recv_sem, in_sem, half_sem, sum_sem,
):
    chips = n // 2
    planes = n // 8
    half = TT * chips
    me = lax.axis_index("sta")
    core = lax.rem(me, 2)
    chip = me // 2
    j = lax.rem(chip, 4)
    plane = me // 8
    odd = lax.rem(j, 2)
    upper = j // 2
    inner = lax.rem((j + 1) // 2, 2)
    peer = me + 1 - 2 * core
    x_dev = me + 2 - 4 * odd
    y_dev = me + 4 - 8 * upper
    z_dev = lax.rem(plane + 1 - 2 * upper + planes, planes) * 8 + lax.rem(me, 8)
    slot_x = 6 - 4 * odd
    slot_v = 2 + 4 * odd
    slot_y = 8 - 8 * upper
    slot_z = 8 * upper
    is0 = core == 0
    is1 = core == 1

    fetches = [
        pltpu.make_async_copy(src, dst, in_sem.at[i])
        for i, (src, dst) in enumerate(
            (
                (rec_hbm, rec), (grn_hbm, grn), (mask_hbm, mask),
                (lists_hbm, lists), (weights_hbm, weights), (tg_hbm, tg),
            )
        )
    ]
    fetches[0].start()
    fetches[1].start()
    barrier = pltpu.get_barrier_semaphore()
    pl.semaphore_signal(barrier, inc=1, device_id=(peer,), device_id_type=MESH)

    @pl.loop(1, chips)
    def _(o):
        other = lax.rem(chip + o, chips) * 2 + core
        pl.semaphore_signal(barrier, inc=1, device_id=(other,), device_id_type=MESH)

    for fetch in fetches[2:]:
        fetch.start()

    def part(ref, q, imag):
        return ref[:, imag * F + q * FC : imag * F + (q + 1) * FC].astype(jnp.float32)

    def fill(q):
        dr, di = part(rec, q, 0), part(rec, q, 1)
        gr, gi = part(grn, q, 0), part(grn, q, 1)
        buf[q, 4, :, 0:FC] = (dr * gr + di * gi).astype(jnp.bfloat16)
        buf[q, 4, :, FC : 2 * FC] = (dr * gi - di * gr).astype(jnp.bfloat16)
        buf[q, 4, :, 2 * FC : 3 * FC] = (gr * gr + gi * gi).astype(jnp.bfloat16)

    def move(q, src, dst, sender, kind, device):
        return pltpu.make_async_remote_copy(
            src_ref=buf.at[q, src], dst_ref=buf.at[q, dst],
            send_sem=send_sem.at[q, sender], recv_sem=recv_sem.at[q, kind],
            device_id=(device,), device_id_type=MESH,
        )

    def relay(q, src, which):
        return move(q, src, src + 2 * core - 1, PEER + which, PEER + which, peer)

    def arrived(q, slot, kind):
        move(q, slot, slot, kind, kind, peer).wait_recv()

    def sent(q, kind):
        move(q, 4, 4, kind, kind, peer).wait_send()

    def send_own(q):
        move(q, 4, slot_z, Y, Y, y_dev).start()
        move(q, 4, slot_v, X, X, x_dev).start()
        relay(q, 4, 0).start()

    def stage1(q):
        arrived(q, slot_y, Y)
        move(q, slot_y, slot_z, Z, Z, z_dev).start()

        @pl.when(core == upper)
        def _():
            relay(q, slot_y, 3).start()

        @pl.when(is0 & (inner == 0))
        def _():
            move(q, slot_y, slot_x, V, V, x_dev).start()

        arrived(q, slot_x, X)

        @pl.when(is1 & (inner == 0))
        def _():
            move(q, slot_x, slot_v, V, V, y_dev).start()

        @pl.when(is1 & (inner == 1))
        def _():
            move(q, slot_x, TRANSIT, V, T, y_dev).start()

        relay(q, slot_x, 1).start()

    def stage2(q):
        @pl.when(is1 & (inner == 0))
        def _():
            arrived(q, TRANSIT, T)
            move(q, TRANSIT, slot_v, T, V, z_dev).start()

        arrived(q, slot_z, Z)

        @pl.when(is0 & (inner == 1))
        def _():
            move(q, slot_z, slot_x, V, V, x_dev).start()

        @pl.when(core != upper)
        def _():
            relay(q, slot_z, 3).start()

    def stage3(q):
        arrived(q, slot_v, V)
        relay(q, slot_v, 2).start()

    def peer_slot(slot):
        return slot + 1 - 2 * core

    def stage4(q):
        arrived(q, peer_slot(4), PEER)
        arrived(q, peer_slot(slot_x), PEER + 1)
        arrived(q, peer_slot(slot_v), PEER + 2)
        theirs = 8 * core
        arrived(q, peer_slot(theirs), PEER + 3)
        window = buf[q, 0:WIN].reshape(WIN * C, 3 * FC)
        sums = jnp.dot(mask_bf[...], window, preferred_element_type=jnp.float32)
        sums = sums * (1.0 / jnp.sqrt(jnp.float32(WIN * C)))
        q_real, q_imag, p = sums[:, :FC], sums[:, FC : 2 * FC], sums[:, 2 * FC :]
        dr, di = part(rec, q, 0), part(rec, q, 1)
        gr, gi = part(grn, q, 0), part(grn, q, 1)
        real = (dr * q_real - di * q_imag - gr * p).astype(jnp.bfloat16)
        imag = (dr * q_imag + di * q_real - gi * p).astype(jnp.bfloat16)
        adj_out[:, q * FC : (q + 1) * FC] = real
        adj_out[:, F + q * FC : F + (q + 1) * FC] = imag
        if q == 0:
            fetches[5].wait()
        more = jnp.dot(
            real, tg[q * FC : (q + 1) * FC, :], preferred_element_type=jnp.float32
        ) + jnp.dot(
            imag, tg[F + q * FC : F + (q + 1) * FC, :], preferred_element_type=jnp.float32
        )
        w_acc[...] = more if q == 0 else w_acc[...] + more

    fetches[0].wait()
    fetches[1].wait()
    fill(0)
    pl.semaphore_wait(barrier, chips)
    send_own(0)
    for q in range(1, Q):
        fill(q)
        if q < AHEAD:
            send_own(q)

    for fetch in fetches[2:5]:
        fetch.wait()
    mask_bf[...] = mask[...].astype(jnp.float32).astype(jnp.bfloat16)
    row = lax.broadcasted_iota(jnp.int32, (2 * half, C), 0)
    late = jnp.where(row >= half, 1, 0)
    rest = row - half * late
    tile = (rest >> 2) * (2 * TT) + late * TT + (rest & 3)
    tile_map = jnp.zeros((2 * half, C), jnp.float32)
    for l in range(lists.shape[0]):
        tile_map = tile_map + jnp.where(lists[l : l + 1, :] == tile, weights[l : l + 1, :], 0.0)
    map_high = tile_map.astype(jnp.bfloat16)
    map_low = (tile_map - map_high.astype(jnp.float32)).astype(jnp.bfloat16)
    map_all[...] = jnp.concatenate([map_high, map_high, map_low], axis=1)

    for step in range(Q + LAGS[2]):
        if step < Q:
            stage1(step)
        if step + AHEAD < Q:
            send_own(step + AHEAD)
        for lag, stage in zip(LAGS, (stage2, stage3, stage4)):
            if 0 <= step - lag < Q:
                stage(step - lag)

    adj_copy = pltpu.make_async_copy(adj_out, adj_hbm, in_sem.at[6])
    adj_copy.start()

    w = w_acc[...]
    w_high = w.astype(jnp.bfloat16)
    w_low = (w - w_high.astype(jnp.float32)).astype(jnp.bfloat16)
    w_all = jnp.concatenate([w_high, w_low, w_high], axis=0)
    terms[...] = jnp.dot(map_all[...], w_all, preferred_element_type=jnp.float32)
    to_peer = pltpu.make_async_remote_copy(
        src_ref=terms.at[pl.ds(pl.multiple_of((1 - core) * half, half), half)], dst_ref=halves,
        send_sem=half_sem.at[0], recv_sem=half_sem.at[1],
        device_id=(peer,), device_id_type=MESH,
    )
    to_peer.start()
    to_peer.wait_recv()
    width = CT // MB

    @pl.loop(0, chips // 2)
    def _(i):
        start = pl.multiple_of(8 * i, 8)
        both = terms[pl.ds(pl.multiple_of(core * half + start, 8), 8), :] + halves[pl.ds(start, 8), :]
        for m in range(MB):
            cols = both[:, m * width : (m + 1) * width]
            wide[2 * i, m * TT : (m + 1) * TT, :] = cols[0:TT]
            wide[2 * i + 1, m * TT : (m + 1) * TT, :] = cols[TT : 2 * TT]
        packed[2 * i] = wide[2 * i].astype(jnp.bfloat16)
        packed[2 * i + 1] = wide[2 * i + 1].astype(jnp.bfloat16)

    def piece(o):
        other = lax.rem(chip + o, chips)
        return pltpu.make_async_remote_copy(
            src_ref=packed.at[other], dst_ref=landed.at[o - 1],
            send_sem=sum_sem.at[0], recv_sem=sum_sem.at[1],
            device_id=(other * 2 + core,), device_id_type=MESH,
        )

    @pl.loop(1, chips)
    def _(o):
        piece(o).start()

    for q in range(Q):
        sent(q, X)
        sent(q, Y)
        sent(q, Z)
        for which in range(4):
            sent(q, PEER + which)

        sent(q, V)

        @pl.when(is1 & (inner == 0))
        def _():
            sent(q, T)

    to_peer.wait_send()
    everything = pltpu.make_async_remote_copy(
        src_ref=packed.at[0 : chips - 1], dst_ref=landed,
        send_sem=sum_sem.at[0], recv_sem=sum_sem.at[1],
        device_id=(peer,), device_id_type=MESH,
    )
    everything.wait_recv()
    total = lax.fori_loop(
        0, chips - 1, lambda o, t: t + landed[o].astype(jnp.float32), wide[chip]
    )
    for m in range(MB):
        ker_out[:, m * width : (m + 1) * width] = total[m * TT : (m + 1) * TT]
    everything.wait_send()
    adj_copy.wait()


def local(n, records, green, pair_mask, tile_lists, tile_weights, tile_green):
    chips = n // 2
    half = TT * chips
    vmem = pl.BlockSpec(memory_space=pltpu.VMEM)
    hbm = pl.BlockSpec(memory_space=pltpu.HBM)
    return pl.pallas_call(
        functools.partial(body, n),
        out_shape=(
            jax.ShapeDtypeStruct((C, 2 * F), jnp.bfloat16),
            jax.ShapeDtypeStruct((TT, CT), jnp.float32),
        ),
        in_specs=[hbm] * 6,
        out_specs=(hbm, vmem),
        scratch_shapes=[
            pltpu.VMEM((C, 2 * F), jnp.bfloat16),
            pltpu.VMEM(records.shape, records.dtype),
            pltpu.VMEM(green.shape, green.dtype),
            pltpu.VMEM(pair_mask.shape, pair_mask.dtype),
            pltpu.VMEM(tile_lists.shape[::-1], tile_lists.dtype),
            pltpu.VMEM(tile_weights.shape[::-1], tile_weights.dtype),
            pltpu.VMEM((Q, WIN + 1, C, 3 * FC), jnp.bfloat16),
            pltpu.VMEM((C, WIN * C), jnp.bfloat16),
            pltpu.VMEM((2 * half, 3 * C), jnp.bfloat16),
            pltpu.VMEM((2 * F, CT), jnp.bfloat16),
            pltpu.VMEM((C, CT), jnp.float32),
            pltpu.VMEM((2 * half, CT), jnp.float32),
            pltpu.VMEM((half, CT), jnp.float32),
            pltpu.VMEM((chips, MB * TT, CT // MB), jnp.float32),
            pltpu.VMEM((chips, MB * TT, CT // MB), jnp.bfloat16),
            pltpu.VMEM((chips - 1, MB * TT, CT // MB), jnp.bfloat16),
            pltpu.SemaphoreType.DMA((Q, KINDS)),
            pltpu.SemaphoreType.DMA((Q, KINDS)),
            pltpu.SemaphoreType.DMA((7,)),
            pltpu.SemaphoreType.DMA((2,)),
            pltpu.SemaphoreType.DMA((2,)),
        ],
        compiler_params=pltpu.CompilerParams(
            collective_id=0, has_side_effects=True, vmem_limit_bytes=56 * 2**20
        ),
        cost_estimate=pl.CostEstimate(flops=10**9, bytes_accessed=6 * 10**6, transcendentals=0),
    )(records, green, pair_mask, tile_lists.T, tile_weights.T, tile_green)


def solution(mesh):
    n = mesh.shape["sta"]
    return jax.shard_map(
        functools.partial(local, n),
        mesh=mesh,
        in_specs=(P("sta", None),) * 6,
        out_specs=(P("sta", None), P("sta", None)),
        check_vma=False,
    )
```

```python
import functools

import jax
import jax.numpy as jnp
from jax import lax
from jax.experimental import pallas as pl
from jax.experimental.pallas import tpu as pltpu
from jax.sharding import PartitionSpec as P

C = 80
F = 1024
TT = 4
WIN = 9
CT = 1024
Q = 8
FC = F // Q
AHEAD = 3
LAGS = 2, 4, 5
MB = 4
MESH = pl.DeviceIdType.MESH

X, Y, Z, V, T, PEER = 0, 1, 2, 3, 4, 5
KINDS = 9
TRANSIT = WIN


def body(
    n, rec_hbm, grn_hbm, mask_hbm, lists_hbm, weights_hbm, tg_hbm, adj_out, ker_out,
    rec, grn, mask, lists, weights, buf, mask_bf, map_all, tg, w_acc, terms, halves, wide, packed, landed,
    send_sem, recv_sem, in_sem, half_sem, sum_sem,
):
    chips = n // 2
    planes = n // 8
    half = TT * chips
    me = lax.axis_index("sta")
    core = lax.rem(me, 2)
    chip = me // 2
    j = lax.rem(chip, 4)
    plane = me // 8
    odd = lax.rem(j, 2)
    upper = j // 2
    inner = lax.rem((j + 1) // 2, 2)
    peer = me + 1 - 2 * core
    x_dev = me + 2 - 4 * odd
    y_dev = me + 4 - 8 * upper
    z_dev = lax.rem(plane + 1 - 2 * upper + planes, planes) * 8 + lax.rem(me, 8)
    slot_x = 6 - 4 * odd
    slot_v = 2 + 4 * odd
    slot_y = 8 - 8 * upper
    slot_z = 8 * upper
    is0 = core == 0
    is1 = core == 1

    fetches = [
        pltpu.make_async_copy(src, dst, in_sem.at[i])
        for i, (src, dst) in enumerate(
            (
                (rec_hbm, rec), (grn_hbm, grn), (mask_hbm, mask),
                (lists_hbm, lists), (weights_hbm, weights), (tg_hbm, tg),
            )
        )
    ]
    fetches[0].start()
    fetches[1].start()
    barrier = pltpu.get_barrier_semaphore()
    pl.semaphore_signal(barrier, inc=1, device_id=(peer,), device_id_type=MESH)

    @pl.loop(1, chips)
    def _(o):
        other = lax.rem(chip + o, chips) * 2 + core
        pl.semaphore_signal(barrier, inc=1, device_id=(other,), device_id_type=MESH)

    for fetch in fetches[2:]:
        fetch.start()

    def part(ref, q, imag):
        return ref[:, imag * F + q * FC : imag * F + (q + 1) * FC].astype(jnp.float32)

    def fill(q):
        dr, di = part(rec, q, 0), part(rec, q, 1)
        gr, gi = part(grn, q, 0), part(grn, q, 1)
        buf[q, 4, :, 0:FC] = (dr * gr + di * gi).astype(jnp.bfloat16)
        buf[q, 4, :, FC : 2 * FC] = (dr * gi - di * gr).astype(jnp.bfloat16)
        buf[q, 4, :, 2 * FC : 3 * FC] = (gr * gr + gi * gi).astype(jnp.bfloat16)

    def move(q, src, dst, sender, kind, device):
        return pltpu.make_async_remote_copy(
            src_ref=buf.at[q, src], dst_ref=buf.at[q, dst],
            send_sem=send_sem.at[q, sender], recv_sem=recv_sem.at[q, kind],
            device_id=(device,), device_id_type=MESH,
        )

    def relay(q, src, which):
        return move(q, src, src + 2 * core - 1, PEER + which, PEER + which, peer)

    def arrived(q, slot, kind):
        move(q, slot, slot, kind, kind, peer).wait_recv()

    def sent(q, kind):
        move(q, 4, 4, kind, kind, peer).wait_send()

    def send_own(q):
        move(q, 4, slot_z, Y, Y, y_dev).start()
        move(q, 4, slot_v, X, X, x_dev).start()
        relay(q, 4, 0).start()

    def stage1(q):
        arrived(q, slot_y, Y)
        move(q, slot_y, slot_z, Z, Z, z_dev).start()

        @pl.when(core == upper)
        def _():
            relay(q, slot_y, 3).start()

        @pl.when(is0 & (inner == 0))
        def _():
            move(q, slot_y, slot_x, V, V, x_dev).start()

        arrived(q, slot_x, X)

        @pl.when(is1 & (inner == 0))
        def _():
            move(q, slot_x, slot_v, V, V, y_dev).start()

        @pl.when(is1 & (inner == 1))
        def _():
            move(q, slot_x, TRANSIT, V, T, y_dev).start()

        relay(q, slot_x, 1).start()

    def stage2(q):
        @pl.when(is1 & (inner == 0))
        def _():
            arrived(q, TRANSIT, T)
            move(q, TRANSIT, slot_v, T, V, z_dev).start()

        arrived(q, slot_z, Z)

        @pl.when(is0 & (inner == 1))
        def _():
            move(q, slot_z, slot_x, V, V, x_dev).start()

        @pl.when(core != upper)
        def _():
            relay(q, slot_z, 3).start()

    def stage3(q):
        arrived(q, slot_v, V)
        relay(q, slot_v, 2).start()

    def peer_slot(slot):
        return slot + 1 - 2 * core

    def stage4(q):
        arrived(q, peer_slot(4), PEER)
        arrived(q, peer_slot(slot_x), PEER + 1)
        arrived(q, peer_slot(slot_v), PEER + 2)
        theirs = 8 * core
        arrived(q, peer_slot(theirs), PEER + 3)
        window = buf[q, 0:WIN].reshape(WIN * C, 3 * FC)
        sums = jnp.dot(mask_bf[...], window, preferred_element_type=jnp.float32)
        sums = sums * (1.0 / jnp.sqrt(jnp.float32(WIN * C)))
        q_real, q_imag, p = sums[:, :FC], sums[:, FC : 2 * FC], sums[:, 2 * FC :]
        dr, di = part(rec, q, 0), part(rec, q, 1)
        gr, gi = part(grn, q, 0), part(grn, q, 1)
        real = (dr * q_real - di * q_imag - gr * p).astype(jnp.bfloat16)
        imag = (dr * q_imag + di * q_real - gi * p).astype(jnp.bfloat16)
        adj_out[:, q * FC : (q + 1) * FC] = real
        adj_out[:, F + q * FC : F + (q + 1) * FC] = imag
        if q == 0:
            fetches[5].wait()
        rows = jnp.concatenate(
            [tg[q * FC : (q + 1) * FC, :], tg[F + q * FC : F + (q + 1) * FC, :]], axis=0
        )
        more = jnp.dot(
            jnp.concatenate([real, imag], axis=1), rows, preferred_element_type=jnp.float32
        )
        w_acc[...] = more if q == 0 else w_acc[...] + more

    fetches[0].wait()
    fetches[1].wait()
    fill(0)
    pl.semaphore_wait(barrier, chips)
    send_own(0)
    for q in range(1, Q):
        fill(q)
        if q < AHEAD:
            send_own(q)

    for fetch in fetches[2:5]:
        fetch.wait()
    mask_bf[...] = mask[...].astype(jnp.float32).astype(jnp.bfloat16)
    row = lax.broadcasted_iota(jnp.int32, (2 * half, C), 0)
    late = jnp.where(row >= half, 1, 0)
    rest = row - half * late
    tile = (rest >> 2) * (2 * TT) + late * TT + (rest & 3)
    tile_map = jnp.zeros((2 * half, C), jnp.float32)
    for l in range(lists.shape[0]):
        tile_map = tile_map + jnp.where(lists[l : l + 1, :] == tile, weights[l : l + 1, :], 0.0)
    map_high = tile_map.astype(jnp.bfloat16)
    map_low = (tile_map - map_high.astype(jnp.float32)).astype(jnp.bfloat16)
    map_all[...] = jnp.concatenate([map_high, map_high, map_low], axis=1)

    for step in range(Q + LAGS[2]):
        if step < Q:
            stage1(step)
        if step + AHEAD < Q:
            send_own(step + AHEAD)
        for lag, stage in zip(LAGS, (stage2, stage3, stage4)):
            if 0 <= step - lag < Q:
                stage(step - lag)

    w = w_acc[...]
    w_high = w.astype(jnp.bfloat16)
    w_low = (w - w_high.astype(jnp.float32)).astype(jnp.bfloat16)
    w_all = jnp.concatenate([w_high, w_low, w_high], axis=0)
    terms[...] = jnp.dot(map_all[...], w_all, preferred_element_type=jnp.float32)
    to_peer = pltpu.make_async_remote_copy(
        src_ref=terms.at[pl.ds(pl.multiple_of((1 - core) * half, half), half)], dst_ref=halves,
        send_sem=half_sem.at[0], recv_sem=half_sem.at[1],
        device_id=(peer,), device_id_type=MESH,
    )
    to_peer.start()
    to_peer.wait_recv()
    width = CT // MB

    @pl.loop(0, chips // 2)
    def _(i):
        start = pl.multiple_of(8 * i, 8)
        both = terms[pl.ds(pl.multiple_of(core * half + start, 8), 8), :] + halves[pl.ds(start, 8), :]
        for m in range(MB):
            cols = both[:, m * width : (m + 1) * width]
            wide[2 * i, m * TT : (m + 1) * TT, :] = cols[0:TT]
            wide[2 * i + 1, m * TT : (m + 1) * TT, :] = cols[TT : 2 * TT]
        packed[2 * i] = wide[2 * i].astype(jnp.bfloat16)
        packed[2 * i + 1] = wide[2 * i + 1].astype(jnp.bfloat16)

    def piece(o):
        other = lax.rem(chip + o, chips)
        return pltpu.make_async_remote_copy(
            src_ref=packed.at[other], dst_ref=landed.at[o - 1],
            send_sem=sum_sem.at[0], recv_sem=sum_sem.at[1],
            device_id=(other * 2 + core,), device_id_type=MESH,
        )

    @pl.loop(1, chips)
    def _(o):
        piece(o).start()

    for q in range(Q):
        sent(q, X)
        sent(q, Y)
        sent(q, Z)
        for which in range(4):
            sent(q, PEER + which)

        sent(q, V)

        @pl.when(is1 & (inner == 0))
        def _():
            sent(q, T)

    to_peer.wait_send()
    everything = pltpu.make_async_remote_copy(
        src_ref=packed.at[0 : chips - 1], dst_ref=landed,
        send_sem=sum_sem.at[0], recv_sem=sum_sem.at[1],
        device_id=(peer,), device_id_type=MESH,
    )
    everything.wait_recv()
    total = lax.fori_loop(
        0, chips - 1, lambda o, t: t + landed[o].astype(jnp.float32), wide[chip]
    )
    for m in range(MB):
        ker_out[:, m * width : (m + 1) * width] = total[m * TT : (m + 1) * TT]
    everything.wait_send()


def local(n, records, green, pair_mask, tile_lists, tile_weights, tile_green):
    chips = n // 2
    half = TT * chips
    vmem = pl.BlockSpec(memory_space=pltpu.VMEM)
    hbm = pl.BlockSpec(memory_space=pltpu.HBM)
    return pl.pallas_call(
        functools.partial(body, n),
        out_shape=(
            jax.ShapeDtypeStruct((C, 2 * F), jnp.bfloat16),
            jax.ShapeDtypeStruct((TT, CT), jnp.float32),
        ),
        in_specs=[hbm] * 6,
        out_specs=(vmem, vmem),
        scratch_shapes=[
            pltpu.VMEM(records.shape, records.dtype),
            pltpu.VMEM(green.shape, green.dtype),
            pltpu.VMEM(pair_mask.shape, pair_mask.dtype),
            pltpu.VMEM(tile_lists.shape[::-1], tile_lists.dtype),
            pltpu.VMEM(tile_weights.shape[::-1], tile_weights.dtype),
            pltpu.VMEM((Q, WIN + 1, C, 3 * FC), jnp.bfloat16),
            pltpu.VMEM((C, WIN * C), jnp.bfloat16),
            pltpu.VMEM((2 * half, 3 * C), jnp.bfloat16),
            pltpu.VMEM((2 * F, CT), jnp.bfloat16),
            pltpu.VMEM((C, CT), jnp.float32),
            pltpu.VMEM((2 * half, CT), jnp.float32),
            pltpu.VMEM((half, CT), jnp.float32),
            pltpu.VMEM((chips, MB * TT, CT // MB), jnp.float32),
            pltpu.VMEM((chips, MB * TT, CT // MB), jnp.bfloat16),
            pltpu.VMEM((chips - 1, MB * TT, CT // MB), jnp.bfloat16),
            pltpu.SemaphoreType.DMA((Q, KINDS)),
            pltpu.SemaphoreType.DMA((Q, KINDS)),
            pltpu.SemaphoreType.DMA((6,)),
            pltpu.SemaphoreType.DMA((2,)),
            pltpu.SemaphoreType.DMA((2,)),
        ],
        compiler_params=pltpu.CompilerParams(
            collective_id=0, has_side_effects=True, vmem_limit_bytes=40 * 2**20
        ),
        cost_estimate=pl.CostEstimate(flops=10**9, bytes_accessed=6 * 10**6, transcendentals=0),
    )(records, green, pair_mask, tile_lists.T, tile_weights.T, tile_green)


def solution(mesh):
    n = mesh.shape["sta"]
    return jax.shard_map(
        functools.partial(local, n),
        mesh=mesh,
        in_specs=(P("sta", None),) * 6,
        out_specs=(P("sta", None), P("sta", None)),
        check_vma=False,
    )
```

```python
import functools

import jax
import jax.numpy as jnp
from jax import lax
from jax.experimental import pallas as pl
from jax.experimental.pallas import tpu as pltpu
from jax.sharding import PartitionSpec as P

C = 80
F = 1024
TT = 4
WIN = 9
CT = 1024
Q = 8
FC = F // Q
AHEAD = 4
LAGS = 3, 5, 6
MB = 4
MESH = pl.DeviceIdType.MESH

X, Y, Z, V, T, PEER = 0, 1, 2, 3, 4, 5
KINDS = 9
TRANSIT = WIN


def body(
    n, rec_hbm, grn_hbm, mask_hbm, lists_hbm, weights_hbm, tg_hbm, adj_out, ker_out,
    rec, grn, mask, lists, weights, buf, mask_bf, map_all, tg, w_acc, terms, halves, wide, packed, landed,
    send_sem, recv_sem, in_sem, half_sem, sum_sem,
):
    chips = n // 2
    planes = n // 8
    half = TT * chips
    me = lax.axis_index("sta")
    core = lax.rem(me, 2)
    chip = me // 2
    j = lax.rem(chip, 4)
    plane = me // 8
    odd = lax.rem(j, 2)
    upper = j // 2
    inner = lax.rem((j + 1) // 2, 2)
    peer = me + 1 - 2 * core
    x_dev = me + 2 - 4 * odd
    y_dev = me + 4 - 8 * upper
    z_dev = lax.rem(plane + 1 - 2 * upper + planes, planes) * 8 + lax.rem(me, 8)
    slot_x = 6 - 4 * odd
    slot_v = 2 + 4 * odd
    slot_y = 8 - 8 * upper
    slot_z = 8 * upper
    is0 = core == 0
    is1 = core == 1

    fetches = [
        pltpu.make_async_copy(src, dst, in_sem.at[i])
        for i, (src, dst) in enumerate(
            (
                (rec_hbm, rec), (grn_hbm, grn), (mask_hbm, mask),
                (lists_hbm, lists), (weights_hbm, weights), (tg_hbm, tg),
            )
        )
    ]
    fetches[0].start()
    fetches[1].start()
    barrier = pltpu.get_barrier_semaphore()
    pl.semaphore_signal(barrier, inc=1, device_id=(peer,), device_id_type=MESH)

    @pl.loop(1, chips)
    def _(o):
        other = lax.rem(chip + o, chips) * 2 + core
        pl.semaphore_signal(barrier, inc=1, device_id=(other,), device_id_type=MESH)

    for fetch in fetches[2:]:
        fetch.start()

    def part(ref, q, imag):
        return ref[:, imag * F + q * FC : imag * F + (q + 1) * FC].astype(jnp.float32)

    def fill(q):
        dr, di = part(rec, q, 0), part(rec, q, 1)
        gr, gi = part(grn, q, 0), part(grn, q, 1)
        buf[q, 4, :, 0:FC] = (dr * gr + di * gi).astype(jnp.bfloat16)
        buf[q, 4, :, FC : 2 * FC] = (dr * gi - di * gr).astype(jnp.bfloat16)
        buf[q, 4, :, 2 * FC : 3 * FC] = (gr * gr + gi * gi).astype(jnp.bfloat16)

    def move(q, src, dst, sender, kind, device):
        return pltpu.make_async_remote_copy(
            src_ref=buf.at[q, src], dst_ref=buf.at[q, dst],
            send_sem=send_sem.at[q, sender], recv_sem=recv_sem.at[q, kind],
            device_id=(device,), device_id_type=MESH,
        )

    def relay(q, src, which):
        return move(q, src, src + 2 * core - 1, PEER + which, PEER + which, peer)

    def arrived(q, slot, kind):
        move(q, slot, slot, kind, kind, peer).wait_recv()

    def sent(q, kind):
        move(q, 4, 4, kind, kind, peer).wait_send()

    def send_own(q):
        move(q, 4, slot_z, Y, Y, y_dev).start()
        move(q, 4, slot_v, X, X, x_dev).start()
        relay(q, 4, 0).start()

    def stage1(q):
        arrived(q, slot_y, Y)
        move(q, slot_y, slot_z, Z, Z, z_dev).start()

        @pl.when(core == upper)
        def _():
            relay(q, slot_y, 3).start()

        @pl.when(is0 & (inner == 0))
        def _():
            move(q, slot_y, slot_x, V, V, x_dev).start()

        arrived(q, slot_x, X)

        @pl.when(is1 & (inner == 0))
        def _():
            move(q, slot_x, slot_v, V, V, y_dev).start()

        @pl.when(is1 & (inner == 1))
        def _():
            move(q, slot_x, TRANSIT, V, T, y_dev).start()

        relay(q, slot_x, 1).start()

    def stage2(q):
        @pl.when(is1 & (inner == 0))
        def _():
            arrived(q, TRANSIT, T)
            move(q, TRANSIT, slot_v, T, V, z_dev).start()

        arrived(q, slot_z, Z)

        @pl.when(is0 & (inner == 1))
        def _():
            move(q, slot_z, slot_x, V, V, x_dev).start()

        @pl.when(core != upper)
        def _():
            relay(q, slot_z, 3).start()

    def stage3(q):
        arrived(q, slot_v, V)
        relay(q, slot_v, 2).start()

    def peer_slot(slot):
        return slot + 1 - 2 * core

    def stage4(q):
        arrived(q, peer_slot(4), PEER)
        arrived(q, peer_slot(slot_x), PEER + 1)
        arrived(q, peer_slot(slot_v), PEER + 2)
        theirs = 8 * core
        arrived(q, peer_slot(theirs), PEER + 3)
        window = buf[q, 0:WIN].reshape(WIN * C, 3 * FC)
        sums = jnp.dot(mask_bf[...], window, preferred_element_type=jnp.float32)
        sums = sums * (1.0 / jnp.sqrt(jnp.float32(WIN * C)))
        q_real, q_imag, p = sums[:, :FC], sums[:, FC : 2 * FC], sums[:, 2 * FC :]
        dr, di = part(rec, q, 0), part(rec, q, 1)
        gr, gi = part(grn, q, 0), part(grn, q, 1)
        real = (dr * q_real - di * q_imag - gr * p).astype(jnp.bfloat16)
        imag = (dr * q_imag + di * q_real - gi * p).astype(jnp.bfloat16)
        adj_out[:, q * FC : (q + 1) * FC] = real
        adj_out[:, F + q * FC : F + (q + 1) * FC] = imag
        if q == 0:
            fetches[5].wait()
        rows = jnp.concatenate(
            [tg[q * FC : (q + 1) * FC, :], tg[F + q * FC : F + (q + 1) * FC, :]], axis=0
        )
        more = jnp.dot(
            jnp.concatenate([real, imag], axis=1), rows, preferred_element_type=jnp.float32
        )
        w_acc[...] = more if q == 0 else w_acc[...] + more

    fetches[0].wait()
    fetches[1].wait()
    fill(0)
    pl.semaphore_wait(barrier, chips)
    send_own(0)
    for q in range(1, Q):
        fill(q)
        if q < AHEAD:
            send_own(q)

    for fetch in fetches[2:5]:
        fetch.wait()
    mask_bf[...] = mask[...].astype(jnp.float32).astype(jnp.bfloat16)
    row = lax.broadcasted_iota(jnp.int32, (2 * half, C), 0)
    late = jnp.where(row >= half, 1, 0)
    rest = row - half * late
    tile = (rest >> 2) * (2 * TT) + late * TT + (rest & 3)
    tile_map = jnp.zeros((2 * half, C), jnp.float32)
    for l in range(lists.shape[0]):
        tile_map = tile_map + jnp.where(lists[l : l + 1, :] == tile, weights[l : l + 1, :], 0.0)
    map_high = tile_map.astype(jnp.bfloat16)
    map_low = (tile_map - map_high.astype(jnp.float32)).astype(jnp.bfloat16)
    map_all[...] = jnp.concatenate([map_high, map_high, map_low], axis=1)

    for step in range(Q + LAGS[2]):
        if step < Q:
            stage1(step)
        if step + AHEAD < Q:
            send_own(step + AHEAD)
        for lag, stage in zip(LAGS, (stage2, stage3, stage4)):
            if 0 <= step - lag < Q:
                stage(step - lag)

    w = w_acc[...]
    w_high = w.astype(jnp.bfloat16)
    w_low = (w - w_high.astype(jnp.float32)).astype(jnp.bfloat16)
    w_all = jnp.concatenate([w_high, w_low, w_high], axis=0)
    terms[...] = jnp.dot(map_all[...], w_all, preferred_element_type=jnp.float32)
    to_peer = pltpu.make_async_remote_copy(
        src_ref=terms.at[pl.ds(pl.multiple_of((1 - core) * half, half), half)], dst_ref=halves,
        send_sem=half_sem.at[0], recv_sem=half_sem.at[1],
        device_id=(peer,), device_id_type=MESH,
    )
    to_peer.start()
    to_peer.wait_recv()
    width = CT // MB

    @pl.loop(0, chips // 2)
    def _(i):
        start = pl.multiple_of(8 * i, 8)
        both = terms[pl.ds(pl.multiple_of(core * half + start, 8), 8), :] + halves[pl.ds(start, 8), :]
        for m in range(MB):
            cols = both[:, m * width : (m + 1) * width]
            wide[2 * i, m * TT : (m + 1) * TT, :] = cols[0:TT]
            wide[2 * i + 1, m * TT : (m + 1) * TT, :] = cols[TT : 2 * TT]
        packed[2 * i] = wide[2 * i].astype(jnp.bfloat16)
        packed[2 * i + 1] = wide[2 * i + 1].astype(jnp.bfloat16)

    def piece(o):
        other = lax.rem(chip + o, chips)
        return pltpu.make_async_remote_copy(
            src_ref=packed.at[other], dst_ref=landed.at[o - 1],
            send_sem=sum_sem.at[0], recv_sem=sum_sem.at[1],
            device_id=(other * 2 + core,), device_id_type=MESH,
        )

    @pl.loop(1, chips)
    def _(o):
        piece(o).start()

    for q in range(Q):
        sent(q, X)
        sent(q, Y)
        sent(q, Z)
        for which in range(4):
            sent(q, PEER + which)

        sent(q, V)

        @pl.when(is1 & (inner == 0))
        def _():
            sent(q, T)

    to_peer.wait_send()
    everything = pltpu.make_async_remote_copy(
        src_ref=packed.at[0 : chips - 1], dst_ref=landed,
        send_sem=sum_sem.at[0], recv_sem=sum_sem.at[1],
        device_id=(peer,), device_id_type=MESH,
    )
    everything.wait_recv()
    total = lax.fori_loop(
        0, chips - 1, lambda o, t: t + landed[o].astype(jnp.float32), wide[chip]
    )
    for m in range(MB):
        ker_out[:, m * width : (m + 1) * width] = total[m * TT : (m + 1) * TT]
    everything.wait_send()


def local(n, records, green, pair_mask, tile_lists, tile_weights, tile_green):
    chips = n // 2
    half = TT * chips
    vmem = pl.BlockSpec(memory_space=pltpu.VMEM)
    hbm = pl.BlockSpec(memory_space=pltpu.HBM)
    return pl.pallas_call(
        functools.partial(body, n),
        out_shape=(
            pltpu.VMEM((C, 2 * F), jnp.bfloat16),
            pltpu.VMEM((TT, CT), jnp.float32),
        ),
        in_specs=[hbm] * 6,
        out_specs=(vmem, vmem),
        scratch_shapes=[
            pltpu.VMEM(records.shape, records.dtype),
            pltpu.VMEM(green.shape, green.dtype),
            pltpu.VMEM(pair_mask.shape, pair_mask.dtype),
            pltpu.VMEM(tile_lists.shape[::-1], tile_lists.dtype),
            pltpu.VMEM(tile_weights.shape[::-1], tile_weights.dtype),
            pltpu.VMEM((Q, WIN + 1, C, 3 * FC), jnp.bfloat16),
            pltpu.VMEM((C, WIN * C), jnp.bfloat16),
            pltpu.VMEM((2 * half, 3 * C), jnp.bfloat16),
            pltpu.VMEM((2 * F, CT), jnp.bfloat16),
            pltpu.VMEM((C, CT), jnp.float32),
            pltpu.VMEM((2 * half, CT), jnp.float32),
            pltpu.VMEM((half, CT), jnp.float32),
            pltpu.VMEM((chips, MB * TT, CT // MB), jnp.float32),
            pltpu.VMEM((chips, MB * TT, CT // MB), jnp.bfloat16),
            pltpu.VMEM((chips - 1, MB * TT, CT // MB), jnp.bfloat16),
            pltpu.SemaphoreType.DMA((Q, KINDS)),
            pltpu.SemaphoreType.DMA((Q, KINDS)),
            pltpu.SemaphoreType.DMA((6,)),
            pltpu.SemaphoreType.DMA((2,)),
            pltpu.SemaphoreType.DMA((2,)),
        ],
        compiler_params=pltpu.CompilerParams(
            collective_id=0, has_side_effects=True, vmem_limit_bytes=40 * 2**20
        ),
        cost_estimate=pl.CostEstimate(flops=10**9, bytes_accessed=6 * 10**6, transcendentals=0),
    )(
        *(
            pltpu.with_memory_space_constraint(value, pltpu.HBM)
            for value in (records, green, pair_mask, tile_lists.T, tile_weights.T, tile_green)
        )
    )


def solution(mesh):
    n = mesh.shape["sta"]
    return jax.shard_map(
        functools.partial(local, n),
        mesh=mesh,
        in_specs=(P("sta", None),) * 6,
        out_specs=(P("sta", None), P("sta", None)),
        check_vma=False,
    )
```

```python
import functools

import jax
import jax.numpy as jnp
from jax import lax
from jax.experimental import pallas as pl
from jax.experimental.pallas import tpu as pltpu
from jax.sharding import PartitionSpec as P

C = 80
F = 1024
TT = 4
WIN = 9
CT = 1024
Q = 8
FC = F // Q
AHEAD = 3
LAGS = 2, 4, 5
MB = 4
MESH = pl.DeviceIdType.MESH

X, Y, Z, V, T, PEER = 0, 1, 2, 3, 4, 5
KINDS = 9
TRANSIT = WIN


def body(
    n, rec_hbm, grn_hbm, mask_hbm, lists_hbm, weights_hbm, tg_hbm, adj_out, ker_out,
    rec, grn, mask, lists, weights, buf, mask_bf, map_all, tg, w_acc, terms, halves, wide, packed, landed,
    send_sem, recv_sem, in_sem, half_sem, sum_sem,
):
    chips = n // 2
    planes = n // 8
    half = TT * chips
    me = lax.axis_index("sta")
    core = lax.rem(me, 2)
    chip = me // 2
    j = lax.rem(chip, 4)
    plane = me // 8
    odd = lax.rem(j, 2)
    upper = j // 2
    inner = lax.rem((j + 1) // 2, 2)
    peer = me + 1 - 2 * core
    x_dev = me + 2 - 4 * odd
    y_dev = me + 4 - 8 * upper
    z_dev = lax.rem(plane + 1 - 2 * upper + planes, planes) * 8 + lax.rem(me, 8)
    slot_x = 6 - 4 * odd
    slot_v = 2 + 4 * odd
    slot_y = 8 - 8 * upper
    slot_z = 8 * upper
    is0 = core == 0
    is1 = core == 1

    fetches = [
        pltpu.make_async_copy(src, dst, in_sem.at[i])
        for i, (src, dst) in enumerate(
            (
                (rec_hbm, rec), (grn_hbm, grn), (mask_hbm, mask),
                (lists_hbm, lists), (weights_hbm, weights), (tg_hbm, tg),
            )
        )
    ]
    fetches[0].start()
    fetches[1].start()
    barrier = pltpu.get_barrier_semaphore()
    pl.semaphore_signal(barrier, inc=1, device_id=(peer,), device_id_type=MESH)

    @pl.loop(1, chips)
    def _(o):
        other = lax.rem(chip + o, chips) * 2 + core
        pl.semaphore_signal(barrier, inc=1, device_id=(other,), device_id_type=MESH)

    for fetch in fetches[2:]:
        fetch.start()

    def part(ref, q, imag):
        return ref[:, imag * F + q * FC : imag * F + (q + 1) * FC].astype(jnp.float32)

    def fill(q):
        dr, di = part(rec, q, 0), part(rec, q, 1)
        gr, gi = part(grn, q, 0), part(grn, q, 1)
        buf[q, 4, :, 0:FC] = (dr * gr + di * gi).astype(jnp.bfloat16)
        buf[q, 4, :, FC : 2 * FC] = (dr * gi - di * gr).astype(jnp.bfloat16)
        buf[q, 4, :, 2 * FC : 3 * FC] = (gr * gr + gi * gi).astype(jnp.bfloat16)

    def move(q, src, dst, sender, kind, device):
        return pltpu.make_async_remote_copy(
            src_ref=buf.at[q, src], dst_ref=buf.at[q, dst],
            send_sem=send_sem.at[q, sender], recv_sem=recv_sem.at[q, kind],
            device_id=(device,), device_id_type=MESH,
        )

    def relay(q, src, which):
        return move(q, src, src + 2 * core - 1, PEER + which, PEER + which, peer)

    def arrived(q, slot, kind):
        move(q, slot, slot, kind, kind, peer).wait_recv()

    def sent(q, kind):
        move(q, 4, 4, kind, kind, peer).wait_send()

    def send_own(q):
        @pl.when(is1)
        def _():
            move(q, 4, slot_v, X, X, x_dev).start()

        move(q, 4, slot_z, Y, Y, y_dev).start()

        @pl.when(is0)
        def _():
            move(q, 4, slot_v, X, X, x_dev).start()

        relay(q, 4, 0).start()

    def stage1(q):
        @pl.when(is1)
        def _():
            arrived(q, slot_x, X)

            @pl.when(inner == 0)
            def _():
                move(q, slot_x, slot_v, V, V, y_dev).start()

            @pl.when(inner == 1)
            def _():
                move(q, slot_x, TRANSIT, V, T, y_dev).start()

        arrived(q, slot_y, Y)
        move(q, slot_y, slot_z, Z, Z, z_dev).start()

        @pl.when(is0 & (inner == 0))
        def _():
            move(q, slot_y, slot_x, V, V, x_dev).start()

        @pl.when(core == upper)
        def _():
            relay(q, slot_y, 3).start()

        @pl.when(is0)
        def _():
            arrived(q, slot_x, X)

        relay(q, slot_x, 1).start()

    def stage2(q):
        @pl.when(is1 & (inner == 0))
        def _():
            arrived(q, TRANSIT, T)
            move(q, TRANSIT, slot_v, T, V, z_dev).start()

        arrived(q, slot_z, Z)

        @pl.when(is0 & (inner == 1))
        def _():
            move(q, slot_z, slot_x, V, V, x_dev).start()

        @pl.when(core != upper)
        def _():
            relay(q, slot_z, 3).start()

    def stage3(q):
        arrived(q, slot_v, V)
        relay(q, slot_v, 2).start()

    def peer_slot(slot):
        return slot + 1 - 2 * core

    def stage4(q):
        arrived(q, peer_slot(4), PEER)
        arrived(q, peer_slot(slot_x), PEER + 1)
        arrived(q, peer_slot(slot_v), PEER + 2)
        theirs = 8 * core
        arrived(q, peer_slot(theirs), PEER + 3)
        window = buf[q, 0:WIN].reshape(WIN * C, 3 * FC)
        sums = jnp.dot(mask_bf[...], window, preferred_element_type=jnp.float32)
        sums = sums * (1.0 / jnp.sqrt(jnp.float32(WIN * C)))
        q_real, q_imag, p = sums[:, :FC], sums[:, FC : 2 * FC], sums[:, 2 * FC :]
        dr, di = part(rec, q, 0), part(rec, q, 1)
        gr, gi = part(grn, q, 0), part(grn, q, 1)
        real = (dr * q_real - di * q_imag - gr * p).astype(jnp.bfloat16)
        imag = (dr * q_imag + di * q_real - gi * p).astype(jnp.bfloat16)
        adj_out[:, q * FC : (q + 1) * FC] = real
        adj_out[:, F + q * FC : F + (q + 1) * FC] = imag
        if q == 0:
            fetches[5].wait()
        rows = jnp.concatenate(
            [tg[q * FC : (q + 1) * FC, :], tg[F + q * FC : F + (q + 1) * FC, :]], axis=0
        )
        more = jnp.dot(
            jnp.concatenate([real, imag], axis=1), rows, preferred_element_type=jnp.float32
        )
        w_acc[...] = more if q == 0 else w_acc[...] + more

    fetches[0].wait()
    fetches[1].wait()
    fill(0)
    pl.semaphore_wait(barrier, chips)
    send_own(0)
    for q in range(1, Q):
        fill(q)
        if q < AHEAD:
            send_own(q)

    for fetch in fetches[2:5]:
        fetch.wait()
    mask_bf[...] = mask[...].astype(jnp.float32).astype(jnp.bfloat16)
    row = lax.broadcasted_iota(jnp.int32, (2 * half, C), 0)
    late = jnp.where(row >= half, 1, 0)
    rest = row - half * late
    tile = (rest >> 2) * (2 * TT) + late * TT + (rest & 3)
    tile_map = jnp.zeros((2 * half, C), jnp.float32)
    for l in range(lists.shape[0]):
        tile_map = tile_map + jnp.where(lists[l : l + 1, :] == tile, weights[l : l + 1, :], 0.0)
    map_high = tile_map.astype(jnp.bfloat16)
    map_low = (tile_map - map_high.astype(jnp.float32)).astype(jnp.bfloat16)
    map_all[...] = jnp.concatenate([map_high, map_high, map_low], axis=1)

    for step in range(Q + LAGS[2]):
        if step < Q:
            stage1(step)
        if step + AHEAD < Q:
            send_own(step + AHEAD)
        for lag, stage in zip(LAGS, (stage2, stage3, stage4)):
            if 0 <= step - lag < Q:
                stage(step - lag)

    w = w_acc[...]
    w_high = w.astype(jnp.bfloat16)
    w_low = (w - w_high.astype(jnp.float32)).astype(jnp.bfloat16)
    w_all = jnp.concatenate([w_high, w_low, w_high], axis=0)
    terms[...] = jnp.dot(map_all[...], w_all, preferred_element_type=jnp.float32)
    to_peer = pltpu.make_async_remote_copy(
        src_ref=terms.at[pl.ds(pl.multiple_of((1 - core) * half, half), half)], dst_ref=halves,
        send_sem=half_sem.at[0], recv_sem=half_sem.at[1],
        device_id=(peer,), device_id_type=MESH,
    )
    to_peer.start()
    to_peer.wait_recv()
    width = CT // MB

    @pl.loop(0, chips // 2)
    def _(i):
        start = pl.multiple_of(8 * i, 8)
        both = terms[pl.ds(pl.multiple_of(core * half + start, 8), 8), :] + halves[pl.ds(start, 8), :]
        for m in range(MB):
            cols = both[:, m * width : (m + 1) * width]
            wide[2 * i, m * TT : (m + 1) * TT, :] = cols[0:TT]
            wide[2 * i + 1, m * TT : (m + 1) * TT, :] = cols[TT : 2 * TT]
        packed[2 * i] = wide[2 * i].astype(jnp.bfloat16)
        packed[2 * i + 1] = wide[2 * i + 1].astype(jnp.bfloat16)

    def piece(o):
        other = lax.rem(chip + o, chips)
        return pltpu.make_async_remote_copy(
            src_ref=packed.at[other], dst_ref=landed.at[o - 1],
            send_sem=sum_sem.at[0], recv_sem=sum_sem.at[1],
            device_id=(other * 2 + core,), device_id_type=MESH,
        )

    @pl.loop(1, chips)
    def _(o):
        piece(o).start()

    for q in range(Q):
        sent(q, X)
        sent(q, Y)
        sent(q, Z)
        for which in range(4):
            sent(q, PEER + which)

        sent(q, V)

        @pl.when(is1 & (inner == 0))
        def _():
            sent(q, T)

    to_peer.wait_send()
    everything = pltpu.make_async_remote_copy(
        src_ref=packed.at[0 : chips - 1], dst_ref=landed,
        send_sem=sum_sem.at[0], recv_sem=sum_sem.at[1],
        device_id=(peer,), device_id_type=MESH,
    )
    everything.wait_recv()
    total = lax.fori_loop(
        0, chips - 1, lambda o, t: t + landed[o].astype(jnp.float32), wide[chip]
    )
    for m in range(MB):
        ker_out[:, m * width : (m + 1) * width] = total[m * TT : (m + 1) * TT]
    everything.wait_send()


def local(n, records, green, pair_mask, tile_lists, tile_weights, tile_green):
    chips = n // 2
    half = TT * chips
    vmem = pl.BlockSpec(memory_space=pltpu.VMEM)
    hbm = pl.BlockSpec(memory_space=pltpu.HBM)
    return pl.pallas_call(
        functools.partial(body, n),
        out_shape=(
            pltpu.VMEM((C, 2 * F), jnp.bfloat16),
            pltpu.VMEM((TT, CT), jnp.float32),
        ),
        in_specs=[hbm] * 6,
        out_specs=(vmem, vmem),
        scratch_shapes=[
            pltpu.VMEM(records.shape, records.dtype),
            pltpu.VMEM(green.shape, green.dtype),
            pltpu.VMEM(pair_mask.shape, pair_mask.dtype),
            pltpu.VMEM(tile_lists.shape[::-1], tile_lists.dtype),
            pltpu.VMEM(tile_weights.shape[::-1], tile_weights.dtype),
            pltpu.VMEM((Q, WIN + 1, C, 3 * FC), jnp.bfloat16),
            pltpu.VMEM((C, WIN * C), jnp.bfloat16),
            pltpu.VMEM((2 * half, 3 * C), jnp.bfloat16),
            pltpu.VMEM((2 * F, CT), jnp.bfloat16),
            pltpu.VMEM((C, CT), jnp.float32),
            pltpu.VMEM((2 * half, CT), jnp.float32),
            pltpu.VMEM((half, CT), jnp.float32),
            pltpu.VMEM((chips, MB * TT, CT // MB), jnp.float32),
            pltpu.VMEM((chips, MB * TT, CT // MB), jnp.bfloat16),
            pltpu.VMEM((chips - 1, MB * TT, CT // MB), jnp.bfloat16),
            pltpu.SemaphoreType.DMA((Q, KINDS)),
            pltpu.SemaphoreType.DMA((Q, KINDS)),
            pltpu.SemaphoreType.DMA((6,)),
            pltpu.SemaphoreType.DMA((2,)),
            pltpu.SemaphoreType.DMA((2,)),
        ],
        compiler_params=pltpu.CompilerParams(
            collective_id=0, has_side_effects=True, vmem_limit_bytes=40 * 2**20
        ),
        cost_estimate=pl.CostEstimate(flops=10**9, bytes_accessed=6 * 10**6, transcendentals=0),
    )(
        *(
            pltpu.with_memory_space_constraint(value, pltpu.HBM)
            for value in (records, green, pair_mask, tile_lists.T, tile_weights.T, tile_green)
        )
    )


def solution(mesh):
    n = mesh.shape["sta"]
    return jax.shard_map(
        functools.partial(local, n),
        mesh=mesh,
        in_specs=(P("sta", None),) * 6,
        out_specs=(P("sta", None), P("sta", None)),
        check_vma=False,
    )
```
